32 devices in a mesh: parts: 2 (over x), space: 16 (over z, y, core).
Axes of the slice: x: 2, y: 2, z: 4, core: 2. Of those that a mesh axis runs over, the one named last changes fastest.
Arguments:
- gas_q: bfloat16 [12288, 512], P(('parts', 'space')), parts along dimension 0, may hold values from -6 to 6
- gas_k: bfloat16 [12288, 512], P(('parts', 'space')), parts along dimension 0, may hold values from -6 to 6
- gas_v: bfloat16 [12288, 512], P(('parts', 'space')), parts along dimension 0, may hold values from -6 to 6
- gas_cotan: bfloat16 [12288, 512], P(('parts', 'space')), parts along dimension 0, may hold values from -6 to 6
- nbr_ids: int32 [96, 16], P('parts'), parts along dimension 0, may hold values from 0 to 47, as said below
- nbr_valid: int32 [96, 16], P('parts'), parts along dimension 0, may hold values from 0 to 1
- if_row: int32 [512], P(('parts', 'space')), parts along dimension 0, may hold values from 0 to 383, as said below
- if_dst: int32 [512], P(('parts', 'space')), parts along dimension 0, may hold values from 0 to 15, as said below
- melt_q: bfloat16 [4096, 512], P(('parts', 'space')), parts along dimension 0, may hold values from -6 to 6
- melt_k: bfloat16 [4096, 512], P(('parts', 'space')), parts along dimension 0, may hold values from -6 to 6
- melt_v: bfloat16 [4096, 512], P(('parts', 'space')), parts along dimension 0, may hold values from -6 to 6
- melt_cotan: bfloat16 [4096, 512], P(('parts', 'space')), parts along dimension 0, may hold values from -6 to 6
Outputs:
- gas_out: bfloat16 [12288, 512], P(('parts', 'space')), parts along dimension 0
- gas_dq: bfloat16 [12288, 512], P(('parts', 'space')), parts along dimension 0
- gas_dk: bfloat16 [12288, 512], P(('parts', 'space')), parts along dimension 0
- gas_dv: bfloat16 [12288, 512], P(('parts', 'space')), parts along dimension 0
- melt_out: bfloat16 [4096, 512], P(('parts', 'space')), parts along dimension 0
- melt_dq: bfloat16 [4096, 512], P(('parts', 'space')), parts along dimension 0
- melt_dk: bfloat16 [4096, 512], P(('parts', 'space')), parts along dimension 0
- melt_dv: bfloat16 [4096, 512], P(('parts', 'space')), parts along dimension 0
The draws below stay inside these ranges and needn't reach their ends.
There are 2 independent parts, one for each index of `parts`. The reference program is written for one: setup_inputs(seed, part) draws one part's arguments, and reference() takes and returns one part's arrays. A program takes and returns all parts, laid end to end along the dimension named above; each array names one. Nothing has to cross between parts.
Inputs may be any that keep to these rules, and one draw needn't show every extreme that they name: `nbr_ids`: for every gas block b the live entries of row b name distinct blocks, b itself among them, all in gas groups within 3 of b's group. For two different gas groups r and o within 3 of each other, the live entries of the blocks of group r name exactly one block of group o. Entries that are not live name any block. `if_row`: the 16 entries of one gas group are distinct. `if_dst`: the 16 entries of one gas group name 8 melt groups, 2 entries each; some melt group is named 2 times by every gas group.
All inputs are finite; a program needn't handle non-finite values.
Results may differ from the reference program's by a relative error of at most 0.012.
The reference program's roundings to bfloat16 on the way count: a program that leaves them out, or rounds other values in their place, can miss the bound.
Values may be sent and summed in bfloat16 or wider, within the bound.
A program may use at most 128 MiB of HBM per device.

```python
import math
import jax
import jax.numpy as jnp
from jax import lax

HEADS = 8
HEAD_DIM = 64
D = 512
BLK = 128
LIST = 16
WIN = 3
ICAP = 2
GB_DEV = 3
MELT_DEV = 128
NBLK = 48
GAS = 6144
MELT = 2048
IF_DEV = 16
IFACE = 256
N_SPACE = 16


def feature_draw(key, row_total, tag):
    base_key = jax.random.fold_in(key, tag)
    return jax.random.truncated_normal(base_key, -5.0, 5.0, (row_total, D), jnp.float32)


def draw_gas_q(key, part):
    return feature_draw(key, GAS, 1).astype(jnp.bfloat16)


def draw_gas_k(key, part):
    return feature_draw(key, GAS, 2).astype(jnp.bfloat16)


def draw_melt_q(key, part):
    return feature_draw(key, MELT, 3).astype(jnp.bfloat16)


def draw_melt_k(key, part):
    return feature_draw(key, MELT, 4).astype(jnp.bfloat16)


def neighbour_tables(key):
    block_index = jnp.arange(NBLK, dtype=jnp.int32)
    reader = block_index // GB_DEV
    offsets = jnp.array([o for o in range(-WIN, WIN + 1) if o != 0], jnp.int32)
    owner_dev = jnp.arange(N_SPACE, dtype=jnp.int32)[:, None] + offsets[None, :]
    inside = (owner_dev >= 0) & (owner_dev < N_SPACE)
    picked = jax.random.randint(jax.random.fold_in(key, 21), (N_SPACE, 2 * WIN), 0, GB_DEV)
    remote = jnp.clip(owner_dev, 0, N_SPACE - 1) * GB_DEV + picked
    local_ids = reader[:, None] * GB_DEV + jnp.arange(GB_DEV, dtype=jnp.int32)[None, :]
    candidates = jnp.concatenate([local_ids, remote[reader]], axis=1)
    col_count = GB_DEV + 2 * WIN
    coin_flip = jax.random.randint(jax.random.fold_in(key, 22), (NBLK, col_count), 0, 4) > 0
    full_block = jax.random.randint(jax.random.fold_in(key, 23), (N_SPACE,), 0, GB_DEV)
    whole_row = block_index % GB_DEV == full_block[reader]
    own_entry = jnp.concatenate([local_ids == block_index[:, None], jnp.zeros((NBLK, 2 * WIN), bool)], axis=1)
    allowed = jnp.concatenate([jnp.ones((NBLK, GB_DEV), bool), inside[reader]], axis=1)
    live_mask = (coin_flip | whole_row[:, None] | own_entry) & allowed
    spare_cols = LIST - col_count
    filler = jax.random.randint(jax.random.fold_in(key, 24), (NBLK, spare_cols), 0, NBLK)
    block_ids = jnp.concatenate([candidates, filler], axis=1)
    live_mask = jnp.concatenate([live_mask, jnp.zeros((NBLK, spare_cols), bool)], axis=1)
    order_score = jax.random.randint(jax.random.fold_in(key, 25), (NBLK, LIST), 0, 1 << 20) * LIST + jnp.arange(LIST)[None, :]
    order_index = jnp.argsort(order_score, axis=1)
    block_ids = jnp.take_along_axis(block_ids, order_index, axis=1)
    live_mask = jnp.take_along_axis(live_mask, order_index, axis=1)
    return (block_ids.astype(jnp.int32), live_mask.astype(jnp.int32))


def draw_nbr_ids(key, part):
    return neighbour_tables(key)[0]


def draw_nbr_valid(key, part):
    return neighbour_tables(key)[1]


def interface_tables(key):
    local_rows = GB_DEV * BLK
    row_score = jax.random.randint(jax.random.fold_in(key, 31), (N_SPACE, local_rows), 0, 1 << 20) * local_rows + jnp.arange(local_rows)[None, :]
    chosen_rows = jnp.argsort(row_score, axis=1)[:, :IF_DEV]
    busy_group = jax.random.randint(jax.random.fold_in(key, 32), (), 0, N_SPACE)
    dest_score = jax.random.randint(jax.random.fold_in(key, 33), (N_SPACE, N_SPACE), 0, 1 << 20) * N_SPACE + jnp.arange(N_SPACE)[None, :]
    dest_score = jnp.where(jnp.arange(N_SPACE)[None, :] == busy_group, -1, dest_score)
    targets = jnp.argsort(dest_score, axis=1)[:, :IF_DEV // ICAP]
    dest_rows = jnp.repeat(targets, ICAP, axis=1)
    mix_score = jax.random.randint(jax.random.fold_in(key, 34), (N_SPACE, IF_DEV), 0, 1 << 20) * IF_DEV + jnp.arange(IF_DEV)[None, :]
    mix_order = jnp.argsort(mix_score, axis=1)
    dest_rows = jnp.take_along_axis(dest_rows, mix_order, axis=1)
    return (chosen_rows.reshape(-1).astype(jnp.int32), dest_rows.reshape(-1).astype(jnp.int32))


def draw_if_row(key, part):
    return interface_tables(key)[0]


def draw_if_dst(key, part):
    return interface_tables(key)[1]


def steps_of(rng, shape, shards, low, high):
    gain, own = 1.0, jax.random.fold_in(rng, 6)
    for dim, blocks in shards:
        heights = jnp.exp(jax.random.uniform(jax.random.fold_in(own, dim), (blocks,), jnp.float32, low / len(shards), high / len(shards)))
        gain = gain * jnp.repeat(heights, shape[dim] // blocks).reshape([-1 if axis == dim else 1 for axis in range(len(shape))])
    return gain


def noise(stream_key, extent, width, bound, pieces=(), kind=jnp.bfloat16):
    result = width * jax.random.normal(stream_key, extent, jnp.float32)
    if pieces:
        result = result * steps_of(stream_key, extent, pieces, -0.22, 0.18)
    return jnp.clip(result, -bound, bound).astype(kind)


def setup_inputs(seed: int = 0, part: int = 0) -> dict:
    key_list = jax.random.split(jax.random.key(seed), 13)
    part_splits = jax.random.split(jax.random.fold_in(key_list[12], part), 13)
    gas_q = draw_gas_q(jax.random.fold_in(jax.random.fold_in(key_list[12], part), 71), part)
    gas_k = draw_gas_k(jax.random.fold_in(jax.random.fold_in(key_list[12], part), 71), part)
    gas_v = noise(part_splits[2], (GAS, D), 1.0, 6.0, ((0, 16),))
    gas_cotan = noise(part_splits[3], (GAS, D), 1.0, 6.0, ((0, 16),))
    nbr_ids = draw_nbr_ids(jax.random.fold_in(jax.random.fold_in(key_list[12], part), 71), part)
    nbr_valid = draw_nbr_valid(jax.random.fold_in(jax.random.fold_in(key_list[12], part), 71), part)
    if_row = draw_if_row(jax.random.fold_in(jax.random.fold_in(key_list[12], part), 71), part)
    if_dst = draw_if_dst(jax.random.fold_in(jax.random.fold_in(key_list[12], part), 71), part)
    melt_q = draw_melt_q(jax.random.fold_in(jax.random.fold_in(key_list[12], part), 71), part)
    melt_k = draw_melt_k(jax.random.fold_in(jax.random.fold_in(key_list[12], part), 71), part)
    melt_v = noise(part_splits[10], (MELT, D), 1.0, 6.0, ((0, 16),))
    melt_cotan = noise(part_splits[11], (MELT, D), 1.0, 6.0, ((0, 16),))
    return dict(gas_q=gas_q, gas_k=gas_k, gas_v=gas_v, gas_cotan=gas_cotan, nbr_ids=nbr_ids, nbr_valid=nbr_valid, if_row=if_row, if_dst=if_dst, melt_q=melt_q, melt_k=melt_k, melt_v=melt_v, melt_cotan=melt_cotan)


MASKED_SCORE = -1e+30

def attend(queries, key_rows, values, cotangent, key_mask):
    row_count = queries.shape[0]
    key_count = key_rows.shape[0]
    query_heads = queries.astype(jnp.float32).reshape(row_count, HEADS, HEAD_DIM)
    key_heads = key_rows.astype(jnp.float32).reshape(key_count, HEADS, HEAD_DIM)
    value_heads = values.astype(jnp.float32).reshape(key_count, HEADS, HEAD_DIM)
    cot_heads = cotangent.astype(jnp.float32).reshape(row_count, HEADS, HEAD_DIM)
    inv_root = 1.0 / math.sqrt(HEAD_DIM)
    scores = jnp.einsum('rhd,shd->hrs', query_heads, key_heads) * inv_root
    scores = jnp.where(key_mask[None, None, :], scores, MASKED_SCORE)
    row_max = lax.optimization_barrier(jnp.max(scores, axis=2, keepdims=True))
    shifted = jnp.exp(scores - row_max)
    weights = shifted / lax.optimization_barrier(jnp.sum(shifted, axis=2, keepdims=True))
    weights_low = lax.optimization_barrier(weights.astype(jnp.bfloat16)).astype(jnp.float32)
    attended = jnp.einsum('hrs,shd->rhd', weights_low, value_heads).reshape(row_count, -1)
    grad_weights = jnp.einsum('rhd,shd->hrs', cot_heads, value_heads)
    row_delta = lax.optimization_barrier(jnp.sum(weights * grad_weights, axis=2, keepdims=True))
    dscore = lax.optimization_barrier((weights * (grad_weights - row_delta)).astype(jnp.bfloat16)).astype(jnp.float32)
    grad_query = jnp.einsum('hrs,shd->rhd', dscore, key_heads).reshape(row_count, -1) * inv_root
    grad_key = jnp.einsum('hrs,rhd->shd', dscore, query_heads).reshape(key_count, -1) * inv_root
    grad_value = jnp.einsum('hrs,rhd->shd', weights_low, cot_heads).reshape(key_count, -1)
    return (attended, grad_query, grad_key, grad_value)

def reference(gas_q, gas_k, gas_v, gas_cotan, nbr_ids, nbr_valid, if_row, if_dst, melt_q, melt_k, melt_v, melt_cotan):
    key_blocks = gas_k.reshape(NBLK, BLK, D)
    value_blocks = gas_v.reshape(NBLK, BLK, D)

    def gas_step(totals, block_index):
        key_total, value_total = totals
        block_ids = nbr_ids[block_index]
        live_mask = nbr_valid[block_index] == 1
        key_rows = key_blocks[block_ids].reshape(LIST * BLK, D)
        value_rows = value_blocks[block_ids].reshape(LIST * BLK, D)
        key_mask = jnp.repeat(live_mask, BLK)
        query_rows = lax.dynamic_slice_in_dim(gas_q, block_index * BLK, BLK, 0)
        cot_rows = lax.dynamic_slice_in_dim(gas_cotan, block_index * BLK, BLK, 0)
        attended, grad_query, grad_key, grad_value = attend(query_rows, key_rows, value_rows, cot_rows, key_mask)
        key_total = key_total.at[block_ids].add(grad_key.reshape(LIST, BLK, D))
        value_total = value_total.at[block_ids].add(grad_value.reshape(LIST, BLK, D))
        return ((key_total, value_total), (attended, grad_query))
    start_total = jnp.zeros((NBLK, BLK, D), jnp.float32)
    (key_total, value_total), (gas_att, gas_gq) = lax.scan(gas_step, (start_total, start_total), jnp.arange(NBLK, dtype=jnp.int32))
    key_flat = key_total.reshape(GAS, D)
    value_flat = value_total.reshape(GAS, D)
    gas_row = jnp.arange(IFACE, dtype=jnp.int32) // IF_DEV * (GB_DEV * BLK) + if_row
    slot_count = N_SPACE * ICAP

    def melt_step(totals, group_index):
        key_acc, value_acc = totals
        belongs = if_dst == group_index
        picked_rows = jnp.argsort(jnp.where(belongs, 0, 1).astype(jnp.int32), stable=True)[:slot_count].astype(jnp.int32)
        in_group = belongs[picked_rows]
        named_rows = gas_row[picked_rows]
        query_rows = lax.dynamic_slice_in_dim(melt_q, group_index * MELT_DEV, MELT_DEV, 0)
        cot_rows = lax.dynamic_slice_in_dim(melt_cotan, group_index * MELT_DEV, MELT_DEV, 0)
        own_keys = lax.dynamic_slice_in_dim(melt_k, group_index * MELT_DEV, MELT_DEV, 0)
        own_values = lax.dynamic_slice_in_dim(melt_v, group_index * MELT_DEV, MELT_DEV, 0)
        key_rows = jnp.concatenate([own_keys, gas_k[named_rows]], axis=0)
        value_rows = jnp.concatenate([own_values, gas_v[named_rows]], axis=0)
        key_mask = jnp.concatenate([jnp.ones((MELT_DEV,), bool), in_group])
        attended, grad_query, grad_key, grad_value = attend(query_rows, key_rows, value_rows, cot_rows, key_mask)
        key_acc = key_acc.at[named_rows].add(jnp.where(in_group[:, None], grad_key[MELT_DEV:], 0.0))
        value_acc = value_acc.at[named_rows].add(jnp.where(in_group[:, None], grad_value[MELT_DEV:], 0.0))
        return ((key_acc, value_acc), (attended, grad_query, grad_key[:MELT_DEV], grad_value[:MELT_DEV]))
    (key_flat, value_flat), (melt_att, melt_gq, melt_gk, melt_gv) = lax.scan(melt_step, (key_flat, value_flat), jnp.arange(N_SPACE, dtype=jnp.int32))
    low = jnp.bfloat16
    return (gas_att.reshape(GAS, D).astype(low), gas_gq.reshape(GAS, D).astype(low), key_flat.astype(low), value_flat.astype(low), melt_att.reshape(MELT, D).astype(low), melt_gq.reshape(MELT, D).astype(low), melt_gk.reshape(MELT, D).astype(low), melt_gv.reshape(MELT, D).astype(low))
```

```python
import functools

import jax
import jax.numpy as jnp
from jax import lax
from jax.experimental import pallas as pl
from jax.experimental.pallas import tpu as pltpu
from jax.sharding import PartitionSpec as P

BLK = 128
LANE = 128
HALF = 64
WIN = 3
ICAP = 2
GB = 3
OFFS = (1, -1, 2, -2, 3, -3)
NOFF = len(OFFS)
CHUNK = 256
PACK = 16
MARK = 1e30
DEAD = 1e30
MESH = pl.DeviceIdType.MESH
F32 = jnp.float32
BF16 = jnp.bfloat16


def iota(shape, dim):
    return lax.broadcasted_iota(jnp.int32, shape, dim)


def onehot(mask):
    return jnp.where(mask, 1.0, 0.0).astype(BF16)


def dot(a, b):
    return jnp.dot(a, b, preferred_element_type=F32)


def dot_nt(a, b):
    return lax.dot_general(a, b, (((1,), (1,)), ((), ())), preferred_element_type=F32)


def any_of(mask):
    hit = jnp.max(jnp.where(mask, 1.0, 0.0), axis=0, keepdims=True)
    return jnp.max(hit, axis=1, keepdims=True)


def split_heads(x, scale):
    lane = iota(x.shape, 1)
    wide = x.astype(F32) * scale
    first = jnp.where(lane < HALF, wide, 0.0).astype(BF16)
    second = jnp.where(lane < HALF, 0.0, wide).astype(BF16)
    return first, second


def kernel(
    n,
    q_ref, k_ref, v_ref, c_ref, ids_ref, val_ref, row_ref, dst_ref, mq_ref, mk_ref, mv_ref, mc_ref,
    o_ref, dq_ref, dk_ref, dv_ref, mo_ref, mdq_ref, mdk_ref, mdv_ref,
    kv, q2, c2, kt, vt, acc, o2, dq2, bias, gsend, gback, grecv, own,
    ipk, irecv, iback, ibrecv, mkv, mbias, iacc,
    gs_sem, gr_sem, bs_sem, br_sem, is_sem, ir_sem, js_sem, jr_sem,
):
    me = lax.axis_index("space")
    rows, width = q_ref.shape
    pairs = width // LANE
    melt = mq_ref.shape[0]
    entries = row_ref.shape[1]
    extra = n * ICAP
    keys = rows + NOFF * BLK

    barrier = pltpu.get_barrier_semaphore()

    @pl.loop(1, n)
    def _(d):
        pl.semaphore_signal(
            barrier, inc=1, device_id={"space": lax.rem(me + d, n)}, device_id_type=MESH
        )

    ids = jnp.where(val_ref[...] == 1, ids_ref[...], -1000)
    block = iota(ids.shape, 0)
    picks = []
    for off in OFFS:
        reader = me + off
        mine = (block >= reader * GB) & (block < reader * GB + GB)
        picks.append([any_of(mine & (ids == me * GB + b)) for b in range(GB)])
    live = []
    for b in range(GB):
        mine = block == me * GB + b
        row = [any_of(mine & (ids == me * GB + s)) for s in range(GB)]
        for off in OFFS:
            owner = me - off
            row.append(any_of(mine & (ids >= owner * GB) & (ids < owner * GB + GB)))
        live.append(row)
    for s in range(GB + NOFF):
        parts = [
            jnp.broadcast_to((1.0 - live[b][s]) * DEAD, (1, BLK)) for b in range(GB)
        ]
        bias[s : s + 1, :] = jnp.concatenate(parts + parts, axis=1)

    for i in range(NOFF):
        for j, ref in enumerate((k_ref, v_ref)):
            picked = sum(
                ref[b * BLK : (b + 1) * BLK, :].astype(F32) * picks[i][b] for b in range(GB)
            ).astype(BF16)
            for p in range(pairs):
                gsend[p, i, j] = picked[:, p * LANE : (p + 1) * LANE]

    e_r, e_c = iota((entries, entries), 0), iota((entries, entries), 1)
    dst_row = dst_ref[...].astype(F32)
    dst_col = jnp.sum(jnp.where(e_r == e_c, dst_row, 0.0), axis=1, keepdims=True)
    row_row = row_ref[...].astype(F32)
    row_col = jnp.sum(jnp.where(e_r == e_c, row_row, 0.0), axis=1, keepdims=True)
    same = dst_row == dst_col
    rank_row = jnp.sum(jnp.where(same & (e_r < e_c), 1.0, 0.0), axis=0, keepdims=True)
    rank_col = jnp.sum(jnp.where(same & (e_c < e_r), 1.0, 0.0), axis=1, keepdims=True)
    place_row = (dst_row * PACK + rank_row).astype(jnp.int32)
    place_col = (dst_col * PACK + rank_col).astype(jnp.int32)
    take = onehot(iota((entries, rows), 1) == row_col.astype(jnp.int32))
    packed = jnp.zeros((n * PACK, LANE), F32)
    count = jnp.zeros((n * PACK, 1), F32)
    slot_iota = iota((n * PACK, entries), 0)
    for j, ref in enumerate((k_ref, v_ref)):
        rows_taken = dot(take, ref[...]).astype(BF16)
        for p in range(pairs):
            hit = slot_iota == place_row + (2 * p + 8 * j)
            packed += dot(onehot(hit), rows_taken[:, p * LANE : (p + 1) * LANE])
            count += jnp.sum(jnp.where(hit, 1.0, 0.0), axis=1, keepdims=True)
    packed = jnp.where(count > 0.5, packed, MARK).astype(BF16)
    ipk[...] = packed.reshape(n, PACK, LANE)

    pl.semaphore_wait(barrier, n - 1)

    def gas_copy(p, i):
        s = rows + i * BLK
        return pltpu.make_async_remote_copy(
            src_ref=gsend.at[p, i],
            dst_ref=kv.at[p, :, pl.ds(s, BLK), :],
            send_sem=gs_sem.at[p, i],
            recv_sem=gr_sem.at[p, i],
            device_id={"space": me + OFFS[i]},
            device_id_type=MESH,
        )

    def back_copy(p, i):
        return pltpu.make_async_remote_copy(
            src_ref=gback.at[p, i],
            dst_ref=grecv.at[p, i],
            send_sem=bs_sem.at[p, i],
            recv_sem=br_sem.at[p, i],
            device_id={"space": me - OFFS[i]},
            device_id_type=MESH,
        )

    def iface_copy(src, dst, ssem, rsem, peer, slot):
        return pltpu.make_async_remote_copy(
            src_ref=src.at[peer],
            dst_ref=dst.at[slot],
            send_sem=ssem.at[peer],
            recv_sem=rsem.at[slot],
            device_id={"space": peer},
            device_id_type=MESH,
        )

    def has(dev):
        return (dev >= 0) & (dev < n)

    def gas_start(p):
        for i, off in enumerate(OFFS):
            @pl.when(has(me + off))
            def _():
                gas_copy(p, i).start()

    gas_start(0)

    @pl.loop(1, n)
    def _(d):
        peer = lax.rem(me + d, n)
        iface_copy(ipk, irecv, is_sem, ir_sem, peer, me).start()

    @pl.loop(1, pairs)
    def _(p):
        gas_start(p)

    irecv[me] = ipk[me]
    for p in range(pairs):
        lanes = slice(p * LANE, (p + 1) * LANE)
        for j, ref in enumerate((k_ref, v_ref)):
            kv[p, j, :rows, :] = ref[:, lanes]
        for j, ref in enumerate((mk_ref, mv_ref)):
            mkv[p, j, :melt, :] = ref[:, lanes]
    for i, off in enumerate(OFFS):
        @pl.when(jnp.logical_not(has(me - off)))
        def _():
            s = rows + i * BLK
            kv[:, :, s : s + BLK, :] = jnp.zeros((pairs, 2, BLK, LANE), BF16)

    def gas_pair(p):
        lanes = pl.ds(pl.multiple_of(p * LANE, LANE), LANE)
        qa, qb = split_heads(q_ref[:, lanes], 0.125)
        q2[:rows, :], q2[rows:, :] = qa, qb
        ca, cb = split_heads(c_ref[:, lanes], 1.0)
        c2[:rows, :], c2[rows:, :] = ca, cb
        for i, off in enumerate(OFFS):
            @pl.when(has(me - off))
            def _():
                gas_copy(p, i).wait_recv()
        kt[...] = kv[p, 0].T
        vt[...] = kv[p, 1].T
        for c in range(2 * rows // CHUNK):
            part = slice(c * CHUNK, (c + 1) * CHUNK)
            qc, cc = q2[part, :], c2[part, :]
            slots = GB + NOFF
            sc = dot_nt(kv[p, 0], qc)
            blk = [sc[s * BLK : (s + 1) * BLK, :] for s in range(slots)]
            pen = [bias[s : s + 1, part] for s in range(slots)]
            top = functools.reduce(
                jnp.maximum,
                [jnp.max(blk[s], axis=0, keepdims=True) - pen[s] for s in range(slots)],
            )
            dp = dot_nt(kv[p, 1], cc)
            ex = [jnp.exp(blk[s] - (top + pen[s])) for s in range(slots)]
            dps = [dp[s * BLK : (s + 1) * BLK, :] for s in range(slots)]
            total = sum(jnp.sum(e, axis=0, keepdims=True) for e in ex)
            inv = 1.0 / total
            delta = inv * sum(
                jnp.sum(e * d, axis=0, keepdims=True) for e, d in zip(ex, dps)
            )
            low, ds = [], []
            for e, d in zip(ex, dps):
                w = e * inv
                low.append(w.astype(BF16))
                ds.append((w * (d - delta)).astype(BF16))
            low = jnp.concatenate(low, axis=0)
            ds = jnp.concatenate(ds, axis=0)
            dv = dot(low, cc)
            dk = dot(ds, qc)
            if c == 0:
                acc[0], acc[1] = dk, dv
            else:
                acc[0] += dk
                acc[1] += dv
            o2[part, :] = dot(vt[...], low).T
            dq2[part, :] = dot(kt[...], ds).T
        lane = iota((rows, LANE), 1)
        o_ref[:, lanes] = jnp.where(lane < HALF, o2[:rows, :], o2[rows:, :]).astype(BF16)
        dq_ref[:, lanes] = (
            jnp.where(lane < HALF, dq2[:rows, :], dq2[rows:, :]) * 0.125
        ).astype(BF16)
        for i, off in enumerate(OFFS):
            s = rows + i * BLK
            gback[p, i] = acc[:, s : s + BLK, :].astype(BF16)

            @pl.when(has(me - off))
            def _():
                back_copy(p, i).start()
        own[p] = acc[:, :rows, :]

    def melt_all():
        @pl.loop(1, n)
        def _(d):
            peer = lax.rem(me + d, n)
            iface_copy(ipk, irecv, is_sem, ir_sem, peer, peer).wait_recv()

        flat = irecv[...].reshape(n * PACK, LANE)
        s_col = iota((extra, n * PACK), 0)
        r_row = iota((extra, n * PACK), 1)
        home = (s_col >> 1) * PACK + (s_col & 1)
        good = None
        for j in range(2):
            for p in range(pairs):
                got = dot(onehot(r_row == home + (2 * p + 8 * j)), flat)
                if good is None:
                    good = jnp.max(got, axis=1, keepdims=True) < 0.1 * MARK
                mkv[p, j, melt:, :] = jnp.where(good, got, 0.0).astype(BF16)
        mbias[:melt, :] = jnp.zeros((melt, LANE), F32)
        mbias[melt:, :] = jnp.broadcast_to(jnp.where(good, 0.0, DEAD), (extra, LANE))
        iacc[...] = jnp.zeros_like(iacc)
        u_row = iota((n * PACK, extra), 0)
        u_col = iota((n * PACK, extra), 1)
        back_home = (u_col >> 1) * PACK + (u_col & 1)

        @pl.loop(0, pairs)
        def _(p):
            lanes = pl.ds(pl.multiple_of(p * LANE, LANE), LANE)
            qc = jnp.concatenate(split_heads(mq_ref[:, lanes], 0.125), axis=0)
            cc = jnp.concatenate(split_heads(mc_ref[:, lanes], 1.0), axis=0)
            kp, vp = mkv[p, 0], mkv[p, 1]
            sc = dot_nt(kp, qc) - mbias[:, :1]
            ex = jnp.exp(sc - jnp.max(sc, axis=0, keepdims=True))
            w = ex * (1.0 / jnp.sum(ex, axis=0, keepdims=True))
            dp = dot_nt(vp, cc)
            delta = jnp.sum(w * dp, axis=0, keepdims=True)
            ds = (w * (dp - delta)).astype(BF16)
            low = w.astype(BF16)
            dv = dot(low, cc)
            dk = dot(ds, qc)
            out = dot(vp.T, low).T
            dq = dot(kp.T, ds).T
            lane = iota((melt, LANE), 1)
            mo_ref[:, lanes] = jnp.where(lane < HALF, out[:melt], out[melt:]).astype(BF16)
            mdq_ref[:, lanes] = (
                jnp.where(lane < HALF, dq[:melt], dq[melt:]) * 0.125
            ).astype(BF16)
            mdk_ref[:, lanes] = dk[:melt].astype(BF16)
            mdv_ref[:, lanes] = dv[:melt].astype(BF16)
            iacc[...] += dot(
                onehot(u_row == back_home + 2 * p), dk[melt:].astype(BF16)
            ) + dot(onehot(u_row == back_home + (2 * p + 8)), dv[melt:].astype(BF16))

        iback[...] = iacc[...].astype(BF16).reshape(n, PACK, LANE)

        @pl.loop(1, n)
        def _(d):
            peer = lax.rem(me + d, n)
            iface_copy(iback, ibrecv, js_sem, jr_sem, peer, me).start()

        ibrecv[me] = iback[me]

    gas_pair(0)
    melt_all()

    @pl.loop(1, pairs)
    def _(p):
        gas_pair(p)

    @pl.loop(0, pairs)
    def _(p):
        for i, off in enumerate(OFFS):
            @pl.when(has(me + off))
            def _():
                back_copy(p, i).wait_recv()
                got = grecv[p, i].astype(F32)
                for b in range(GB):
                    own[p, :, b * BLK : (b + 1) * BLK, :] += got * picks[i][b]

    @pl.loop(1, n)
    def _(d):
        peer = lax.rem(me + d, n)
        iface_copy(iback, ibrecv, js_sem, jr_sem, peer, peer).wait_recv()

    flat = ibrecv[...].reshape(n * PACK, LANE)
    put = onehot(iota((rows, entries), 0) == row_row.astype(jnp.int32))
    slot_lane = iota((entries, n * PACK), 1)
    for j, ref in enumerate((dk_ref, dv_ref)):
        for p in range(pairs):
            mine = dot(onehot(slot_lane == place_col + (2 * p + 8 * j)), flat).astype(BF16)
            ref[:, p * LANE : (p + 1) * LANE] = (own[p, j] + dot(put, mine)).astype(BF16)

    @pl.loop(0, pairs)
    def _(p):
        for i, off in enumerate(OFFS):
            @pl.when(has(me + off))
            def _():
                gas_copy(p, i).wait_send()

            @pl.when(has(me - off))
            def _():
                back_copy(p, i).wait_send()

    @pl.loop(1, n)
    def _(d):
        peer = lax.rem(me + d, n)
        iface_copy(ipk, irecv, is_sem, ir_sem, peer, me).wait_send()
        iface_copy(iback, ibrecv, js_sem, jr_sem, peer, me).wait_send()


def local(n, *args):
    q, k, v, c, ids, val, if_row, if_dst, mq, mk, mv, mc = args
    rows, width = q.shape
    melt = mq.shape[0]
    pairs = width // LANE
    keys = rows + NOFF * BLK
    extra = n * ICAP
    dma = pltpu.SemaphoreType.DMA
    vmem = pl.BlockSpec(memory_space=pltpu.VMEM)
    gas_out = jax.ShapeDtypeStruct((rows, width), BF16)
    melt_out = jax.ShapeDtypeStruct((melt, width), BF16)
    heads = width // HALF
    pieces = heads * (rows * keys + melt * (melt + extra))
    return pl.pallas_call(
        functools.partial(kernel, n),
        out_shape=[gas_out] * 4 + [melt_out] * 4,
        in_specs=[vmem] * 12,
        out_specs=[vmem] * 8,
        scratch_shapes=[
            pltpu.VMEM((pairs, 2, keys, LANE), BF16),
            pltpu.VMEM((2 * rows, LANE), BF16),
            pltpu.VMEM((2 * rows, LANE), BF16),
            pltpu.VMEM((LANE, keys), BF16),
            pltpu.VMEM((LANE, keys), BF16),
            pltpu.VMEM((2, keys, LANE), F32),
            pltpu.VMEM((2 * rows, LANE), F32),
            pltpu.VMEM((2 * rows, LANE), F32),
            pltpu.VMEM((16, 2 * rows), F32),
            pltpu.VMEM((pairs, NOFF, 2, BLK, LANE), BF16),
            pltpu.VMEM((pairs, NOFF, 2, BLK, LANE), BF16),
            pltpu.VMEM((pairs, NOFF, 2, BLK, LANE), BF16),
            pltpu.VMEM((pairs, 2, rows, LANE), F32),
            pltpu.VMEM((n, PACK, LANE), BF16),
            pltpu.VMEM((n, PACK, LANE), BF16),
            pltpu.VMEM((n, PACK, LANE), BF16),
            pltpu.VMEM((n, PACK, LANE), BF16),
            pltpu.VMEM((pairs, 2, melt + extra, LANE), BF16),
            pltpu.VMEM((melt + extra, LANE), F32),
            pltpu.VMEM((n * PACK, LANE), F32),
            dma((pairs, NOFF)),
            dma((pairs, NOFF)),
            dma((pairs, NOFF)),
            dma((pairs, NOFF)),
            dma((n,)),
            dma((n,)),
            dma((n,)),
            dma((n,)),
        ],
        compiler_params=pltpu.CompilerParams(
            collective_id=0, has_side_effects=True, vmem_limit_bytes=48 * 2**20
        ),
        cost_estimate=pl.CostEstimate(
            flops=pieces * HALF * 10,
            bytes_accessed=16 * width * (rows + melt),
            transcendentals=pieces,
        ),
    )(q, k, v, c, ids, val, if_row.reshape(1, -1), if_dst.reshape(1, -1), mq, mk, mv, mc)


def solution(mesh):
    both = P(("parts", "space"), None)
    flat = P(("parts", "space"))
    listed = P("parts", None)
    return jax.shard_map(
        functools.partial(local, mesh.shape["space"]),
        mesh=mesh,
        in_specs=(both, both, both, both, listed, listed, flat, flat, both, both, both, both),
        out_specs=(both,) * 8,
        check_vma=False,
    )
```

```python
import functools

import jax
import jax.numpy as jnp
from jax import lax
from jax.experimental import pallas as pl
from jax.experimental.pallas import tpu as pltpu
from jax.sharding import PartitionSpec as P

BLK = 128
LANE = 128
HALF = 64
WIN = 3
ICAP = 2
GB = 3
OFFS = (1, -1, 2, -2, 3, -3)
NOFF = len(OFFS)
CHUNK = 256
PACK = 16
MARK = 1e30
DEAD = 1e30
MESH = pl.DeviceIdType.MESH
F32 = jnp.float32
BF16 = jnp.bfloat16


def iota(shape, dim):
    return lax.broadcasted_iota(jnp.int32, shape, dim)


def onehot(mask):
    return jnp.where(mask, 1.0, 0.0).astype(BF16)


def dot(a, b):
    return jnp.dot(a, b, preferred_element_type=F32)


def dot_nt(a, b):
    return lax.dot_general(a, b, (((1,), (1,)), ((), ())), preferred_element_type=F32)


def any_of(mask):
    hit = jnp.max(jnp.where(mask, 1.0, 0.0), axis=0, keepdims=True)
    return jnp.max(hit, axis=1, keepdims=True)


def split_heads(x, scale):
    lane = iota(x.shape, 1)
    wide = x.astype(F32) * scale
    first = jnp.where(lane < HALF, wide, 0.0).astype(BF16)
    second = jnp.where(lane < HALF, 0.0, wide).astype(BF16)
    return first, second


def kernel(
    n,
    q_hbm, k_hbm, v_hbm, c_hbm, ids_hbm, val_hbm, row_hbm, dst_hbm, mq_hbm, mk_hbm, mv_hbm, mc_hbm,
    o_ref, dq_ref, dk_ref, dv_ref, mo_ref, mdq_ref, mdk_ref, mdv_ref,
    q_ref, k_ref, v_ref, c_ref, ids_ref, val_ref, row_ref, dst_ref, mq_ref, mk_ref, mv_ref, mc_ref,
    in_sem, kv, q2, c2, kt, vt, acc, o2, dq2, bias, gsend, gback, grecv, own,
    ipk, irecv, iback, ibrecv, mkv, mbias, iacc,
    gs_sem, gr_sem, bs_sem, br_sem, is_sem, ir_sem, js_sem, jr_sem,
):
    me = lax.axis_index("space")
    loads = [
        pltpu.make_async_copy(src, dst, in_sem.at[i])
        for i, (src, dst) in enumerate(
            (
                (ids_hbm, ids_ref), (val_hbm, val_ref), (k_hbm, k_ref), (v_hbm, v_ref),
                (row_hbm, row_ref), (dst_hbm, dst_ref), (mk_hbm, mk_ref), (mv_hbm, mv_ref),
                (q_hbm, q_ref), (c_hbm, c_ref), (mq_hbm, mq_ref), (mc_hbm, mc_ref),
            )
        )
    ]
    for load in loads:
        load.start()
    rows, width = q_ref.shape
    pairs = width // LANE
    melt = mq_ref.shape[0]
    entries = row_ref.shape[1]
    extra = n * ICAP
    keys = rows + NOFF * BLK

    barrier = pltpu.get_barrier_semaphore()

    @pl.loop(1, n)
    def _(d):
        pl.semaphore_signal(
            barrier, inc=1, device_id={"space": lax.rem(me + d, n)}, device_id_type=MESH
        )

    for load in loads[:2]:
        load.wait()

    ids = jnp.where(val_ref[...] == 1, ids_ref[...], -1000)
    block = iota(ids.shape, 1)
    picks = []
    for off in OFFS:
        reader = me + off
        mine = (block >= reader * GB) & (block < reader * GB + GB)
        picks.append([any_of(mine & (ids == me * GB + b)) for b in range(GB)])
    def gas_copy(p, i):
        s = rows + i * BLK
        return pltpu.make_async_remote_copy(
            src_ref=gsend.at[p, i],
            dst_ref=kv.at[p, :, pl.ds(s, BLK), :],
            send_sem=gs_sem.at[p, i],
            recv_sem=gr_sem.at[p, i],
            device_id={"space": me + OFFS[i]},
            device_id_type=MESH,
        )

    def back_copy(p, i):
        return pltpu.make_async_remote_copy(
            src_ref=gback.at[p, i],
            dst_ref=grecv.at[p, i],
            send_sem=bs_sem.at[p, i],
            recv_sem=br_sem.at[p, i],
            device_id={"space": me - OFFS[i]},
            device_id_type=MESH,
        )

    def iface_copy(src, dst, ssem, rsem, peer, slot):
        return pltpu.make_async_remote_copy(
            src_ref=src.at[peer],
            dst_ref=dst.at[slot],
            send_sem=ssem.at[peer],
            recv_sem=rsem.at[slot],
            device_id={"space": peer},
            device_id_type=MESH,
        )

    def has(dev):
        return (dev >= 0) & (dev < n)

    def gas_start(p):
        lanes = pl.ds(pl.multiple_of(p * LANE, LANE), LANE)
        for i, off in enumerate(OFFS):
            for j, ref in enumerate((k_ref, v_ref)):
                gsend[p, i, j] = sum(
                    ref[b * BLK : (b + 1) * BLK, lanes].astype(F32) * picks[i][b]
                    for b in range(GB)
                ).astype(BF16)

            @pl.when(has(me + off))
            def _():
                gas_copy(p, i).start()

    for load in loads[2:4]:
        load.wait()
    pl.semaphore_wait(barrier, n - 1)

    @pl.loop(0, 2)
    def _(p):
        gas_start(p)

    for load in loads[4:6]:
        load.wait()
    e_r, e_c = iota((entries, entries), 0), iota((entries, entries), 1)
    dst_row = dst_ref[...].astype(F32)
    dst_col = jnp.sum(jnp.where(e_r == e_c, dst_row, 0.0), axis=1, keepdims=True)
    row_row = row_ref[...].astype(F32)
    row_col = jnp.sum(jnp.where(e_r == e_c, row_row, 0.0), axis=1, keepdims=True)
    same = dst_row == dst_col
    rank_row = jnp.sum(jnp.where(same & (e_r < e_c), 1.0, 0.0), axis=0, keepdims=True)
    rank_col = jnp.sum(jnp.where(same & (e_c < e_r), 1.0, 0.0), axis=1, keepdims=True)
    place_row = (dst_row * PACK + rank_row).astype(jnp.int32)
    place_col = (dst_col * PACK + rank_col).astype(jnp.int32)
    take = onehot(iota((entries, rows), 1) == row_col.astype(jnp.int32))
    packed = jnp.zeros((n * PACK, LANE), F32)
    used = jnp.zeros((n * PACK, entries), F32)
    slot_iota = iota((n * PACK, entries), 0)
    for j, ref in enumerate((k_ref, v_ref)):
        rows_taken = dot(take, ref[...]).astype(BF16)
        for p in range(pairs):
            hit = slot_iota == place_row + (2 * p + 8 * j)
            packed += dot(onehot(hit), rows_taken[:, p * LANE : (p + 1) * LANE])
            used += jnp.where(hit, 1.0, 0.0)
    count = jnp.sum(used, axis=1, keepdims=True)
    packed = jnp.where(count > 0.5, packed, MARK).astype(BF16)
    ipk[...] = packed.reshape(n, PACK, LANE)

    @pl.loop(1, n)
    def _(d):
        peer = lax.rem(me + d, n)
        iface_copy(ipk, irecv, is_sem, ir_sem, peer, me).start()

    @pl.loop(2, pairs)
    def _(p):
        gas_start(p)

    live = []
    for b in range(GB):
        mine = block == me * GB + b
        row = [any_of(mine & (ids == me * GB + s)) for s in range(GB)]
        for off in OFFS:
            owner = me - off
            row.append(any_of(mine & (ids >= owner * GB) & (ids < owner * GB + GB)))
        live.append(row)
    for s in range(GB + NOFF):
        parts = [
            jnp.broadcast_to((1.0 - live[b][s]) * DEAD, (1, BLK)) for b in range(GB)
        ]
        bias[s : s + 1, :] = jnp.concatenate(parts + parts, axis=1)

    for load in loads[6:]:
        load.wait()
    irecv[me] = ipk[me]
    for p in range(pairs):
        lanes = slice(p * LANE, (p + 1) * LANE)
        for j, ref in enumerate((k_ref, v_ref)):
            kv[p, j, :rows, :] = ref[:, lanes]
        for j, ref in enumerate((mk_ref, mv_ref)):
            mkv[p, j, :melt, :] = ref[:, lanes]
    for i, off in enumerate(OFFS):
        @pl.when(jnp.logical_not(has(me - off)))
        def _():
            s = rows + i * BLK
            kv[:, :, s : s + BLK, :] = jnp.zeros((pairs, 2, BLK, LANE), BF16)

    def gas_pair(p):
        lanes = pl.ds(pl.multiple_of(p * LANE, LANE), LANE)
        qa, qb = split_heads(q_ref[:, lanes], 0.125)
        q2[:rows, :], q2[rows:, :] = qa, qb
        ca, cb = split_heads(c_ref[:, lanes], 1.0)
        c2[:rows, :], c2[rows:, :] = ca, cb
        for i, off in enumerate(OFFS):
            @pl.when(has(me - off))
            def _():
                gas_copy(p, i).wait_recv()
        kt[...] = kv[p, 0].T
        vt[...] = kv[p, 1].T
        for c in range(2 * rows // CHUNK):
            part = slice(c * CHUNK, (c + 1) * CHUNK)
            qc, cc = q2[part, :], c2[part, :]
            slots = GB + NOFF
            sc = dot_nt(kv[p, 0], qc)
            blk = [sc[s * BLK : (s + 1) * BLK, :] for s in range(slots)]
            pen = [bias[s : s + 1, part] for s in range(slots)]
            top = functools.reduce(
                jnp.maximum,
                [jnp.max(blk[s], axis=0, keepdims=True) - pen[s] for s in range(slots)],
            )
            dp = dot_nt(kv[p, 1], cc)
            ex = [jnp.exp(blk[s] - (top + pen[s])) for s in range(slots)]
            dps = [dp[s * BLK : (s + 1) * BLK, :] for s in range(slots)]
            total = sum(jnp.sum(e, axis=0, keepdims=True) for e in ex)
            inv = 1.0 / total
            delta = inv * sum(
                jnp.sum(e * d, axis=0, keepdims=True) for e, d in zip(ex, dps)
            )
            low, ds = [], []
            for e, d in zip(ex, dps):
                w = e * inv
                low.append(w.astype(BF16))
                ds.append((w * (d - delta)).astype(BF16))
            low = jnp.concatenate(low, axis=0)
            ds = jnp.concatenate(ds, axis=0)
            dv = dot(low, cc)
            dk = dot(ds, qc)
            if c == 0:
                acc[0], acc[1] = dk, dv
            else:
                acc[0] += dk
                acc[1] += dv
            o2[part, :] = dot(vt[...], low).T
            dq2[part, :] = dot(kt[...], ds).T
        lane = iota((rows, LANE), 1)
        o_ref[:, lanes] = jnp.where(lane < HALF, o2[:rows, :], o2[rows:, :]).astype(BF16)
        dq_ref[:, lanes] = (
            jnp.where(lane < HALF, dq2[:rows, :], dq2[rows:, :]) * 0.125
        ).astype(BF16)
        for i, off in enumerate(OFFS):
            s = rows + i * BLK
            gback[p, i] = acc[:, s : s + BLK, :].astype(BF16)

            @pl.when(has(me - off))
            def _():
                back_copy(p, i).start()
        own[p] = acc[:, :rows, :]

    def melt_all():
        @pl.loop(1, n)
        def _(d):
            peer = lax.rem(me + d, n)
            iface_copy(ipk, irecv, is_sem, ir_sem, peer, peer).wait_recv()

        flat = irecv[...].reshape(n * PACK, LANE)
        s_col = iota((extra, n * PACK), 0)
        r_row = iota((extra, n * PACK), 1)
        home = (s_col >> 1) * PACK + (s_col & 1)
        good = None
        for j in range(2):
            for p in range(pairs):
                got = dot(onehot(r_row == home + (2 * p + 8 * j)), flat)
                if good is None:
                    good = jnp.max(got, axis=1, keepdims=True) < 0.1 * MARK
                mkv[p, j, melt:, :] = jnp.where(good, got, 0.0).astype(BF16)
        mbias[:melt, :] = jnp.zeros((melt, LANE), F32)
        mbias[melt:, :] = jnp.broadcast_to(jnp.where(good, 0.0, DEAD), (extra, LANE))
        iacc[...] = jnp.zeros_like(iacc)
        u_row = iota((n * PACK, extra), 0)
        u_col = iota((n * PACK, extra), 1)
        back_home = (u_col >> 1) * PACK + (u_col & 1)

        @pl.loop(0, pairs)
        def _(p):
            lanes = pl.ds(pl.multiple_of(p * LANE, LANE), LANE)
            qc = jnp.concatenate(split_heads(mq_ref[:, lanes], 0.125), axis=0)
            cc = jnp.concatenate(split_heads(mc_ref[:, lanes], 1.0), axis=0)
            kp, vp = mkv[p, 0], mkv[p, 1]
            sc = dot_nt(kp, qc) - mbias[:, :1]
            ex = jnp.exp(sc - jnp.max(sc, axis=0, keepdims=True))
            w = ex * (1.0 / jnp.sum(ex, axis=0, keepdims=True))
            dp = dot_nt(vp, cc)
            delta = jnp.sum(w * dp, axis=0, keepdims=True)
            ds = (w * (dp - delta)).astype(BF16)
            low = w.astype(BF16)
            dv = dot(low, cc)
            dk = dot(ds, qc)
            out = dot(vp.T, low).T
            dq = dot(kp.T, ds).T
            lane = iota((melt, LANE), 1)
            mo_ref[:, lanes] = jnp.where(lane < HALF, out[:melt], out[melt:]).astype(BF16)
            mdq_ref[:, lanes] = (
                jnp.where(lane < HALF, dq[:melt], dq[melt:]) * 0.125
            ).astype(BF16)
            mdk_ref[:, lanes] = dk[:melt].astype(BF16)
            mdv_ref[:, lanes] = dv[:melt].astype(BF16)
            iacc[...] += dot(
                onehot(u_row == back_home + 2 * p), dk[melt:].astype(BF16)
            ) + dot(onehot(u_row == back_home + (2 * p + 8)), dv[melt:].astype(BF16))

        iback[...] = iacc[...].astype(BF16).reshape(n, PACK, LANE)

        @pl.loop(1, n)
        def _(d):
            peer = lax.rem(me + d, n)
            iface_copy(iback, ibrecv, js_sem, jr_sem, peer, me).start()

        ibrecv[me] = iback[me]

    @pl.loop(0, 2)
    def _(p):
        gas_pair(p)

    melt_all()

    @pl.loop(2, pairs)
    def _(p):
        gas_pair(p)

    @pl.loop(1, n)
    def _(d):
        peer = lax.rem(me + d, n)
        iface_copy(iback, ibrecv, js_sem, jr_sem, peer, peer).wait_recv()

    flat = ibrecv[...].reshape(n * PACK, LANE)
    put = onehot(iota((rows, entries), 0) == row_row.astype(jnp.int32))
    slot_lane = iota((entries, n * PACK), 1)

    @pl.loop(0, pairs)
    def _(p):
        for j in range(2):
            mine = dot(onehot(slot_lane == place_col + (2 * p + 8 * j)), flat).astype(BF16)
            own[p, j] += dot(put, mine)

    @pl.loop(0, pairs)
    def _(p):
        lanes = pl.ds(pl.multiple_of(p * LANE, LANE), LANE)
        for i, off in enumerate(OFFS):
            @pl.when(has(me + off))
            def _():
                back_copy(p, i).wait_recv()
                got = grecv[p, i].astype(F32)
                for b in range(GB):
                    own[p, :, b * BLK : (b + 1) * BLK, :] += got * picks[i][b]
        dk_ref[:, lanes] = own[p, 0].astype(BF16)
        dv_ref[:, lanes] = own[p, 1].astype(BF16)

    @pl.loop(0, pairs)
    def _(p):
        for i, off in enumerate(OFFS):
            @pl.when(has(me + off))
            def _():
                gas_copy(p, i).wait_send()

            @pl.when(has(me - off))
            def _():
                back_copy(p, i).wait_send()

    @pl.loop(1, n)
    def _(d):
        peer = lax.rem(me + d, n)
        iface_copy(ipk, irecv, is_sem, ir_sem, peer, me).wait_send()
        iface_copy(iback, ibrecv, js_sem, jr_sem, peer, me).wait_send()


def store(*refs):
    sems = refs[-1]
    copies = [pltpu.make_async_copy(refs[i], refs[8 + i], sems.at[i]) for i in range(8)]
    for copy in copies:
        copy.start()
    for copy in copies:
        copy.wait()


def local(n, *args):
    q, k, v, c, ids, val, if_row, if_dst, mq, mk, mv, mc = args
    rows, width = q.shape
    melt = mq.shape[0]
    pairs = width // LANE
    keys = rows + NOFF * BLK
    extra = n * ICAP
    dma = pltpu.SemaphoreType.DMA
    vmem = pl.BlockSpec(memory_space=pltpu.VMEM)
    ins = (
        q, k, v, c, ids.T, val.T, if_row.reshape(1, -1), if_dst.reshape(1, -1), mq, mk, mv, mc
    )
    gas_out = jax.ShapeDtypeStruct((rows, width), BF16)
    melt_out = jax.ShapeDtypeStruct((melt, width), BF16)
    heads = width // HALF
    pieces = heads * (rows * keys + melt * (melt + extra))
    outs = pl.pallas_call(
        functools.partial(kernel, n),
        out_shape=[gas_out] * 4 + [melt_out] * 4,
        in_specs=[pl.BlockSpec(memory_space=pltpu.HBM)] * 12,
        out_specs=[vmem] * 8,
        scratch_shapes=[
            *[pltpu.VMEM(x.shape, x.dtype) for x in ins],
            dma((len(ins),)),
            pltpu.VMEM((pairs, 2, keys, LANE), BF16),
            pltpu.VMEM((2 * rows, LANE), BF16),
            pltpu.VMEM((2 * rows, LANE), BF16),
            pltpu.VMEM((LANE, keys), BF16),
            pltpu.VMEM((LANE, keys), BF16),
            pltpu.VMEM((2, keys, LANE), F32),
            pltpu.VMEM((2 * rows, LANE), F32),
            pltpu.VMEM((2 * rows, LANE), F32),
            pltpu.VMEM((16, 2 * rows), F32),
            pltpu.VMEM((pairs, NOFF, 2, BLK, LANE), BF16),
            pltpu.VMEM((pairs, NOFF, 2, BLK, LANE), BF16),
            pltpu.VMEM((pairs, NOFF, 2, BLK, LANE), BF16),
            pltpu.VMEM((pairs, 2, rows, LANE), F32),
            pltpu.VMEM((n, PACK, LANE), BF16),
            pltpu.VMEM((n, PACK, LANE), BF16),
            pltpu.VMEM((n, PACK, LANE), BF16),
            pltpu.VMEM((n, PACK, LANE), BF16),
            pltpu.VMEM((pairs, 2, melt + extra, LANE), BF16),
            pltpu.VMEM((melt + extra, LANE), F32),
            pltpu.VMEM((n * PACK, LANE), F32),
            dma((pairs, NOFF)),
            dma((pairs, NOFF)),
            dma((pairs, NOFF)),
            dma((pairs, NOFF)),
            dma((n,)),
            dma((n,)),
            dma((n,)),
            dma((n,)),
        ],
        compiler_params=pltpu.CompilerParams(
            collective_id=0, has_side_effects=True, vmem_limit_bytes=62 * 2**20
        ),
        cost_estimate=pl.CostEstimate(
            flops=pieces * HALF * 10,
            bytes_accessed=16 * width * (rows + melt),
            transcendentals=pieces,
        ),
    )(*ins)
    return pl.pallas_call(
        store,
        out_shape=[gas_out] * 4 + [melt_out] * 4,
        in_specs=[vmem] * 8,
        out_specs=[pl.BlockSpec(memory_space=pltpu.HBM)] * 8,
        scratch_shapes=[dma((8,))],
        compiler_params=pltpu.CompilerParams(vmem_limit_bytes=62 * 2**20),
    )(*outs)


def solution(mesh):
    both = P(("parts", "space"), None)
    flat = P(("parts", "space"))
    listed = P("parts", None)
    return jax.shard_map(
        functools.partial(local, mesh.shape["space"]),
        mesh=mesh,
        in_specs=(both, both, both, both, listed, listed, flat, flat, both, both, both, both),
        out_specs=(both,) * 8,
        check_vma=False,
    )
```
